256 devices in a mesh: member: 16 (over z_hi, x, core), ctx: 16 (over y, z_lo).
Axes of the slice: x: 4, y: 4, z: 8 (z_hi: 2, z_lo: 4; z = z_hi * 4 + z_lo), core: 2. Of those that a mesh axis runs over, the one named last changes fastest.
Arguments:
- queries: bfloat16 [16, 2048, 4096], P('member', 'ctx'), may hold values from -8 to 8
- response_keys: bfloat16 [16, 2048, 512], P('member', 'ctx'), may hold values from -4.5 to 4.5
- response_values: bfloat16 [16, 2048, 512], P('member', 'ctx'), may hold values from -16 to 16
- prompt_keys: bfloat16 [512, 512], P(('member', 'ctx')), may hold values from -4.5 to 4.5
- prompt_values: bfloat16 [512, 512], P(('member', 'ctx')), may hold values from -16 to 16
- block_offsets: int32 [16, 16], P('member'), may hold values from 0 to 15, each once within a row
- lengths: int32 [16], P('member'), may hold values from 512 to 2048, as said below
Outputs:
- attended: bfloat16 [16, 2048, 4096], P('member', 'ctx')
The draws below stay inside these ranges and needn't reach their ends.
Inputs may be any that keep to these rules, and one draw needn't show every extreme that they name: `lengths`: each response has from 512 to 2048 valid slab tokens; some response has exactly 2048, some exactly 512. `block_offsets`: each row of a response's blocks names every block once.
All inputs are finite; a program needn't handle non-finite values.
Results may differ from the reference program's by a relative error of at most 0.0065.
Values may be sent and summed in bfloat16 or wider, within the bound.
No kernel may reach another device: no remote copies, remote signals or barrier semaphores. Data moves between devices by JAX's collectives and lax.ppermute only.
A program may use at most 128 MiB of HBM per device.

```python
import math
import jax
import jax.numpy as jnp
from jax import lax

H = 32
KVH = 4
HD = 128
TOK_DEV = 128
MEMBERS = 16
SLAB = 2048
PROMPT = 512
N_CTX = 16


def draw_queries(key, part):
    key = jax.random.fold_in(key, 1)
    layout = (MEMBERS, SLAB, H * HD)
    drawn = jnp.clip(2.0 * jax.random.normal(key, layout, jnp.float32), -8.0, 8.0)
    return drawn.astype(jnp.bfloat16)


def draw_prompt_keys(key, part):
    key = jax.random.fold_in(key, 2)
    layout = (PROMPT, KVH * HD)
    drawn = jnp.clip(jax.random.normal(key, layout, jnp.float32), -4.5, 4.5)
    return drawn.astype(jnp.bfloat16)


def draw_response_keys(key, part):
    key = jax.random.fold_in(key, 3)
    layout = (MEMBERS, SLAB, KVH * HD)
    drawn = jnp.clip(jax.random.normal(key, layout, jnp.float32), -4.5, 4.5)
    return drawn.astype(jnp.bfloat16)


def draw_lengths(key, part):
    key = jax.random.fold_in(key, 4)
    drawn = jax.random.randint(jax.random.fold_in(key, 1), (MEMBERS,), SLAB // 4, SLAB + 1)
    chosen = jax.random.randint(jax.random.fold_in(key, 2), (), 0, MEMBERS)
    member_ids = jnp.arange(MEMBERS)
    drawn = jnp.where(member_ids == chosen, SLAB, drawn)
    drawn = jnp.where(member_ids == (chosen + 1) % MEMBERS, SLAB // 4, drawn)
    return drawn.astype(jnp.int32)


def shard_levels(key, shape, cuts, least, high):
    loudness, own = 1.0, jax.random.fold_in(key, 6)
    for position, blocks in cuts:
        draws = jnp.exp(jax.random.uniform(jax.random.fold_in(own, position), (blocks,), jnp.float32, least / len(cuts), high / len(cuts)))
        loudness = loudness * jnp.repeat(draws, shape[position] // blocks).reshape([-1 if axis == position else 1 for axis in range(len(shape))])
    return loudness


def gaussian(key, dims, scale, bound, pieces=(), kind=jnp.bfloat16):
    gain = shard_levels(key, dims, pieces, -0.22, 0.18) if pieces else 1.0
    result = jax.random.normal(key, dims, jnp.float32) * scale * gain
    return jnp.minimum(jnp.maximum(result, -bound), bound).astype(kind)


def setup_inputs(seed: int = 0) -> dict:
    keys = jax.random.split(jax.random.key(seed), 8)
    queries = draw_queries(jax.random.fold_in(keys[7], 71), 0)
    response_keys = draw_response_keys(jax.random.fold_in(keys[7], 71), 0)
    response_values = gaussian(keys[2], (MEMBERS, SLAB, KVH * HD), 4.0, 16.0, ((0, 16), (1, 16)))
    prompt_keys = draw_prompt_keys(jax.random.fold_in(keys[7], 71), 0)
    prompt_values = gaussian(keys[4], (PROMPT, KVH * HD), 4.0, 16.0, ((0, 256),))
    block_offsets = jax.vmap(lambda own: jax.random.permutation(own, N_CTX))(jax.random.split(keys[5], MEMBERS)).reshape((MEMBERS, N_CTX)).astype(jnp.int32)
    lengths = draw_lengths(jax.random.fold_in(keys[7], 71), 0)
    return dict(queries=queries, response_keys=response_keys, response_values=response_values, prompt_keys=prompt_keys, prompt_values=prompt_values, block_offsets=block_offsets, lengths=lengths)


def one_response(member_inputs, prompt_keys, prompt_values):
    member_queries, member_keys, member_values, member_offsets, valid_length = member_inputs
    row_ids = jnp.arange(SLAB, dtype=jnp.int32)
    positions = member_offsets[row_ids // TOK_DEV].astype(jnp.int32) * TOK_DEV + row_ids % TOK_DEV
    causal = (positions[None, :] <= positions[:, None]) & (positions[None, :] < valid_length)
    visible = jnp.concatenate([jnp.ones((SLAB, PROMPT), dtype=bool), causal], axis=1)
    group_size = H // KVH
    all_keys = jnp.concatenate([prompt_keys, member_keys], axis=0).astype(jnp.float32)
    all_values = jnp.concatenate([prompt_values, member_values], axis=0).astype(jnp.float32)
    key_heads = jnp.transpose(all_keys.reshape(PROMPT + SLAB, KVH, HD), (1, 0, 2))
    value_heads = jnp.transpose(all_values.reshape(PROMPT + SLAB, KVH, HD), (1, 0, 2))
    query_heads = jnp.transpose(member_queries.astype(jnp.float32).reshape(SLAB, KVH, group_size, HD), (1, 2, 0, 3))
    score_scale = 1.0 / math.sqrt(HD)

    def one_head(head_inputs):
        head_queries, head_keys, head_values = head_inputs
        scores = jnp.einsum('ntd,sd->nts', head_queries, head_keys) * score_scale
        scores = jnp.where(visible[None], scores, -jnp.inf)
        row_max = lax.optimization_barrier(jnp.max(scores, axis=-1, keepdims=True))
        exponent = jnp.exp(scores - row_max)
        totals = lax.optimization_barrier(jnp.sum(exponent, axis=-1))
        weights = lax.optimization_barrier(exponent.astype(jnp.bfloat16))
        summed = jnp.einsum('nts,sd->ntd', weights.astype(jnp.float32), head_values)
        return summed / totals[..., None]
    outputs = lax.map(one_head, (query_heads, key_heads, value_heads))
    outputs = jnp.transpose(outputs, (2, 0, 1, 3)).reshape(SLAB, H * HD)
    return outputs.astype(jnp.bfloat16)

def reference(queries, response_keys, response_values, prompt_keys, prompt_values, block_offsets, lengths):

    def per_member(member_inputs):
        return one_response(member_inputs, prompt_keys, prompt_values)
    return lax.map(per_member, (queries, response_keys, response_values, block_offsets, lengths))
```

```python
import math

import jax
import jax.numpy as jnp
from jax import lax
from jax.experimental import pallas as pl
from jax.experimental.pallas import tpu as pltpu
from jax.sharding import PartitionSpec as P

HD = 128
KV_HEADS = 4
GROUP = 8
TOK = 128
PAIR = 2
SCALE = math.log2(math.e) / math.sqrt(HD)
NEG = -1e30
AXES = ("member", "ctx")


def moves(step):
    pairs = []
    for i in range(256):
        zh, x, c, y, z = i // 128, i // 32 % 4, i // 16 % 2, i // 4 % 4, i % 4
        zh2, x2, c2, y2, z2 = step(zh, x, c, y, z)
        pairs.append((i, (((zh2 * 4 + x2) * 2 + c2) * 4 + y2) * 4 + z2))
    return pairs


Z_STEPS = [moves(lambda zh, x, c, y, z, k=k: (zh, x, c, y, z ^ (1, 2)[c ^ k])) for k in (0, 1)]
Y_STEPS = [moves(lambda zh, x, c, y, z, k=k: (zh, x, c, y ^ (1, 3)[c ^ k], z)) for k in (0, 1)]
X_STEPS = [moves(lambda zh, x, c, y, z, k=k: (zh, x ^ (1, 3)[c ^ k], c, y, z)) for k in (0, 1)]
ZH_STEP = moves(lambda zh, x, c, y, z: (zh ^ 1, x, c, y, z))
CORE_STEP = moves(lambda zh, x, c, y, z: (zh, x, c ^ 1, y, z))


def send(value, pairs):
    return lax.ppermute(value, AXES, pairs)


def double(value, pairs):
    return jnp.concatenate([value, send(value, pairs)], axis=0)


def make_kernel(counts):
    prompt_rows = 512
    keys = prompt_rows + TOK * sum(counts)

    def kernel(offsets, length, q_ref, pk_ref, pv_ref, *refs):
        n = len(counts)
        k_refs, v_refs = refs[:n], refs[n : 2 * n]
        out_ref, k_aug, v_aug = refs[2 * n :]
        ctx, member = lax.axis_index("ctx"), lax.axis_index("member")
        core = member % 2
        y, z = ctx // 4, ctx % 4

        @pl.when(pl.program_id(0) == 0)
        def _():
            v_aug[:, HD:] = jnp.ones((keys, HD), jnp.bfloat16)
            k_aug[:prompt_rows, HD:] = jnp.zeros((prompt_rows, HD), jnp.bfloat16)
            q_pos = lax.broadcasted_iota(jnp.int32, (TOK, TOK), 1) + offsets[0, ctx] * TOK
            k_row = lax.broadcasted_iota(jnp.int32, (TOK, TOK), 0)
            for index, (ybits, zbits) in enumerate(BLOCKS):
                dy = block_delta(ybits, core, 1, 3)
                dz = block_delta(zbits, core, 1, 2)
                source = (y ^ dy) * 4 + (z ^ dz)
                k_pos = k_row + offsets[0, source] * TOK
                counted = (k_pos <= q_pos) & (k_pos < length[0])
                start = prompt_rows + index * TOK
                k_aug[start : start + TOK, HD:] = jnp.where(counted, 0.0, NEG).astype(jnp.bfloat16)

        k_aug[:prompt_rows, :HD] = pk_ref[...].reshape(prompt_rows, HD)
        v_aug[:prompt_rows, :HD] = pv_ref[...].reshape(prompt_rows, HD)
        start = prompt_rows
        for i in range(n):
            rows = counts[i] * TOK
            k_aug[start : start + rows, :HD] = k_refs[i][...].reshape(rows, HD)
            v_aug[start : start + rows, :HD] = v_refs[i][...].reshape(rows, HD)
            start += rows
        eye = (
            lax.broadcasted_iota(jnp.int32, (TOK, TOK), 0)
            == lax.broadcasted_iota(jnp.int32, (TOK, TOK), 1)
        )
        eye = jnp.where(eye, 1.0, 0.0).astype(jnp.bfloat16)
        keys_all, values_all = k_aug[...], v_aug[...]

        def score(h):
            rows = [
                jnp.concatenate([q_ref[:, (h * PAIR + u) * HD : (h * PAIR + u + 1) * HD], eye], axis=1)
                for u in range(PAIR)
            ]
            return lax.dot_general(
                jnp.concatenate(rows, axis=0),
                keys_all,
                (((1,), (1,)), ((), ())),
                preferred_element_type=jnp.float32,
            )

        def finish(h, s):
            top = jnp.max(s, axis=1, keepdims=True) * SCALE
            weights = jnp.exp2(s * SCALE - top).astype(jnp.bfloat16)
            both = lax.dot_general(
                weights, values_all, (((1,), (0,)), ((), ())), preferred_element_type=jnp.float32
            )
            result = (both[:, :HD] / both[:, HD:]).astype(jnp.bfloat16)
            for u in range(PAIR):
                out_ref[:, (h * PAIR + u) * HD : (h * PAIR + u + 1) * HD] = result[u * TOK : (u + 1) * TOK]

        s = score(0)
        for h in range(GROUP // PAIR):
            ahead = score(h + 1) if h + 1 < GROUP // PAIR else None
            finish(h, s)
            s = ahead

    return kernel


def block_delta(bits, core, first, second):
    step0 = first + core * (second - first)
    step1 = second + core * (first - second)
    return (step0 if bits & 1 else 0) ^ (step1 if bits & 2 else 0)


BLOCKS = [(yb, zb) for yb in range(4) for zb in (0, 1)] + [(yb, zb) for yb in range(4) for zb in (2, 3)]


def attend(offsets, length, q, prompt, groups):
    counts = [g.shape[0] for g in groups]
    keys = 512 + TOK * sum(counts)
    in_specs = [
        pl.BlockSpec(memory_space=pltpu.SMEM),
        pl.BlockSpec(memory_space=pltpu.SMEM),
        pl.BlockSpec((TOK, GROUP * HD), lambda g: (0, g)),
        pl.BlockSpec((None, 512, HD), lambda g: (0, 0, g)),
        pl.BlockSpec((None, 512, HD), lambda g: (1, 0, g)),
    ]
    for part in (0, 1):
        for n in counts:
            in_specs.append(pl.BlockSpec((n, None, TOK, HD), lambda g, part=part: (0, part, 0, g)))
    return pl.pallas_call(
        make_kernel(counts),
        grid=(KV_HEADS,),
        in_specs=in_specs,
        out_specs=pl.BlockSpec((TOK, GROUP * HD), lambda g: (0, g)),
        out_shape=jax.ShapeDtypeStruct((TOK, KV_HEADS * GROUP * HD), jnp.bfloat16),
        scratch_shapes=[pltpu.VMEM((keys, 2 * HD), jnp.bfloat16)] * 2,
        compiler_params=pltpu.CompilerParams(vmem_limit_bytes=48 << 20),
        cost_estimate=pl.CostEstimate(
            flops=4 * 4096 * keys * HD, bytes_accessed=8 << 20, transcendentals=4096 * keys
        ),
        name="attend",
    )(offsets, length, q, prompt, prompt, *groups, *groups)


def body(
    queries, response_keys, response_values, prompt_keys, prompt_values, block_offsets, lengths
):
    own = jnp.concatenate([response_keys, response_values], axis=0)[None]
    prompt = jnp.concatenate([prompt_keys[None], prompt_values[None]], axis=0)[None]
    near = double(own, Z_STEPS[0])
    far = send(near, Z_STEPS[1])
    for pairs in Y_STEPS:
        near = double(near, pairs)
    for pairs in Y_STEPS:
        far = double(far, pairs)
    for pairs in (Z_STEPS[0], Z_STEPS[1], ZH_STEP, Y_STEPS[0], Y_STEPS[1], X_STEPS[0], X_STEPS[1], CORE_STEP):
        prompt = double(prompt, pairs)
    prompt = prompt.transpose(1, 0, 2, 3).reshape(2, 512, KV_HEADS * HD)
    out = attend(block_offsets, lengths, queries[0], prompt, (near, far))
    return out[None]


def solution(mesh):
    return jax.shard_map(
        body,
        mesh=mesh,
        in_specs=(
            P("member", "ctx", None),
            P("member", "ctx", None),
            P("member", "ctx", None),
            P(("member", "ctx"), None),
            P(("member", "ctx"), None),
            P("member", None),
            P("member"),
        ),
        out_specs=P("member", "ctx", None),
        check_vma=False,
    )
```

```python
import math

import jax
import jax.numpy as jnp
from jax import lax
from jax.experimental import pallas as pl
from jax.experimental.pallas import tpu as pltpu
from jax.sharding import PartitionSpec as P

HD = 128
KV_HEADS = 4
GROUP = 8
WIDE = GROUP * HD
TOK = 128
RIDE = 16
PAIR = 2
PAIRS = GROUP // PAIR
SCALE = math.log2(math.e) / math.sqrt(HD)
NEG = -1e30
GROUPS = ([3], [1], [2], [0])
AXES = ("member", "ctx")
VMEM = pl.BlockSpec(memory_space=pltpu.VMEM)
SMEM = pl.BlockSpec(memory_space=pltpu.SMEM)


def moves(step):
    pairs = []
    for i in range(256):
        zh, x, c, y, z = i // 128, i // 32 % 4, i // 16 % 2, i // 4 % 4, i % 4
        zh2, x2, c2, y2, z2 = step(zh, x, c, y, z)
        pairs.append((i, (((zh2 * 4 + x2) * 2 + c2) * 4 + y2) * 4 + z2))
    return pairs


Z_STEPS = [moves(lambda zh, x, c, y, z, k=k: (zh, x, c, y, z ^ (1, 2)[c ^ k])) for k in (0, 1)]
Z_STEPS.append(moves(lambda zh, x, c, y, z: (zh, x, c, y, z ^ 3)))
Y_STEPS = [moves(lambda zh, x, c, y, z, k=k: (zh, x, c, y ^ (1, 3)[c ^ k], z)) for k in (0, 1)]
Y_STEPS.append(moves(lambda zh, x, c, y, z: (zh, x, c, y ^ 2, z)))
X_STEPS = [moves(lambda zh, x, c, y, z, k=k: (zh, x ^ (1, 3)[c ^ k], c, y, z)) for k in (0, 1)]
X_STEPS.append(moves(lambda zh, x, c, y, z: (zh, x ^ 2, c, y, z)))
ZH_STEP = moves(lambda zh, x, c, y, z: (zh ^ 1, x, c, y, z))
CORE_STEP = moves(lambda zh, x, c, y, z: (zh, x, c ^ 1, y, z))


def send(value, pairs):
    return lax.ppermute(value, AXES, pairs)


def join(*values):
    return jnp.concatenate(values, axis=0)


def double(value, pairs):
    return join(value, send(value, pairs))


def place():
    ctx, member = lax.axis_index("ctx"), lax.axis_index("member")
    return member % 2, ctx // 4, ctx % 4


def delta(bits, core, first, second):
    step0 = first + core * (second - first)
    step1 = second + core * (first - second)
    return (step0 if bits & 1 else 0) ^ (step1 if bits & 2 else 0)


def head_of(bits):
    core, y, _ = place()
    return y ^ delta(bits, core, 1, 3)


def columns(head, width):
    return pl.ds(pl.multiple_of(head * width, width), width)


def two_rows(pair):
    row = lax.broadcasted_iota(jnp.int32, (RIDE, HD), 0)
    wide = pair.astype(jnp.float32)
    return jnp.where(row == 0, wide[:1], jnp.where(row == 1, wide[1:], 0.0)).astype(jnp.bfloat16)


def split_kv_kernel(k_ref, v_ref, pk_ref, pv_ref, *outs):
    for bits in range(4):
        part = columns(head_of(bits), HD)
        outs[bits][:TOK, :HD] = k_ref[:, part]
        outs[bits][:TOK, HD:] = v_ref[:, part]
        outs[bits][TOK:, :HD] = two_rows(pk_ref[:, part])
        outs[bits][TOK:, HD:] = two_rows(pv_ref[:, part])


def split_kv(keys, values, prompt_keys, prompt_values):
    return pl.pallas_call(
        split_kv_kernel,
        in_specs=[VMEM] * 4,
        out_specs=[VMEM] * 4,
        out_shape=[jax.ShapeDtypeStruct((TOK + RIDE, 2 * HD), jnp.bfloat16)] * 4,
        name="split_kv",
    )(keys, values, prompt_keys, prompt_values)


def split_q_kernel(q_ref, *outs):
    for bits in range(4):
        outs[bits][...] = q_ref[:, columns(head_of(bits), WIDE)]


def split_q(q):
    return pl.pallas_call(
        split_q_kernel,
        in_specs=[VMEM],
        out_specs=[VMEM] * 4,
        out_shape=[jax.ShapeDtypeStruct((TOK, WIDE), jnp.bfloat16)] * 4,
        name="split_q",
    )(q)


def merge_kernel(*refs):
    out_ref = refs[4]
    for bits in range(4):
        out_ref[:, columns(head_of(bits), WIDE)] = refs[bits][...]


def merge(parts):
    return pl.pallas_call(
        merge_kernel,
        in_specs=[VMEM] * 4,
        out_specs=VMEM,
        out_shape=jax.ShapeDtypeStruct((TOK, KV_HEADS * WIDE), jnp.bfloat16),
        name="merge",
    )(*parts)


def make_kernel(queries, sizes, blocks, carried, last):
    keys = TOK * len(blocks)
    count = len(queries)

    def kernel(offsets, length, *refs):
        q_refs, refs = refs[:count], refs[count:]
        pieces, refs = refs[: len(sizes)], refs[len(sizes) :]
        if carried:
            stat_in, sum_in, refs = refs[:count], refs[count : 2 * count], refs[2 * count :]
        if last:
            outs, refs = refs[:count], refs[count:]
        else:
            stat_out, sum_out, mark_ref = refs[:count], refs[count : 2 * count], refs[2 * count]
            refs = refs[2 * count + 1 :]
            mark_ref[...] = jnp.zeros(mark_ref.shape, jnp.float32)
        k_aug, v_aug = refs
        core, y, z = place()
        token = lax.broadcasted_iota(jnp.int32, (TOK, TOK), 1)
        k_row = lax.broadcasted_iota(jnp.int32, (TOK, TOK), 0)
        for index, bits in enumerate(blocks):
            to = slice(index * TOK, (index + 1) * TOK)
            if bits is not None:
                source = (y ^ delta(bits[0], core, 1, 3)) * 4 + (z ^ delta(bits[1], core, 1, 2))
                k_pos = k_row + offsets[0, source] * TOK
            for i in range(count):
                if bits is None:
                    bias = jnp.zeros((TOK, TOK), jnp.bfloat16)
                else:
                    q_pos = token + offsets[0, (y ^ delta(queries[i], core, 1, 3)) * 4 + z] * TOK
                    counted = (k_pos <= q_pos) & (k_pos < length[0])
                    bias = jnp.where(counted, 0.0, NEG).astype(jnp.bfloat16)
                k_aug[i, to, HD:] = bias
        v_aug[:, HD:] = jnp.ones((keys, HD), jnp.bfloat16)
        start = 0
        for piece, size in zip(pieces, sizes):
            v_aug[start : start + size, :HD] = piece[:, HD:]
            for i in range(count):
                k_aug[i, start : start + size, :HD] = piece[:, :HD]
            start += size
        eye = jnp.where(token == k_row, 1.0, 0.0).astype(jnp.bfloat16)
        low = lax.broadcasted_iota(jnp.int32, (1, HD), 1) < HD // 2

        def score(i, h):
            heads = [
                jnp.concatenate([q_refs[i][:, (h * PAIR + u) * HD : (h * PAIR + u + 1) * HD], eye], axis=1)
                for u in range(PAIR)
            ]
            return lax.dot_general(
                jnp.concatenate(heads, axis=0),
                k_aug[i],
                (((1,), (1,)), ((), ())),
                preferred_element_type=jnp.float32,
            )

        def finish(i, h, s):
            top = jnp.max(s, axis=1, keepdims=True)
            if carried:
                stat = stat_in[i][h]
                before = jnp.max(jnp.where(low, stat, -3e38), axis=1, keepdims=True)
                total = jnp.max(jnp.where(low, -3e38, stat), axis=1, keepdims=True)
                top = jnp.maximum(before, top)
                rescale = jnp.exp2((before - top) * SCALE)
            weights = jnp.exp2(s * SCALE - top * SCALE).astype(jnp.bfloat16)
            both = lax.dot_general(
                weights, v_aug[...], (((1,), (0,)), ((), ())), preferred_element_type=jnp.float32
            )
            weighted, totals = both[:, :HD], both[:, HD:]
            if carried:
                weighted = weighted + sum_in[i][h] * rescale
                totals = totals + total * rescale
            if last:
                result = (weighted / totals).astype(jnp.bfloat16)
                for u in range(PAIR):
                    outs[i][:, (h * PAIR + u) * HD : (h * PAIR + u + 1) * HD] = result[u * TOK : (u + 1) * TOK]
            else:
                stat_out[i][h] = jnp.where(low, top, totals)
                sum_out[i][h] = weighted

        steps = [(i, h) for i in range(count) for h in range(PAIRS)]
        s = score(*steps[0])
        for n, step in enumerate(steps):
            ahead = score(*steps[n + 1]) if n + 1 < len(steps) else None
            finish(*step, s)
            s = ahead

    return kernel


def attend(offsets, length, queries, q, pieces, blocks, carry=(), last=False):
    sizes = [p.shape[0] for p in pieces]
    keys, count = TOK * len(blocks), len(queries)
    state = jax.ShapeDtypeStruct((PAIRS, PAIR * TOK, HD), jnp.float32)
    result = jax.ShapeDtypeStruct((TOK, WIDE), jnp.bfloat16)
    mark = jax.ShapeDtypeStruct((8, HD), jnp.float32)
    outs = [result] * count if last else [state] * (2 * count) + [mark]
    return pl.pallas_call(
        make_kernel(queries, sizes, blocks, bool(carry), last),
        in_specs=[SMEM, SMEM] + [VMEM] * (count + len(pieces) + len(carry)),
        out_specs=[VMEM] * len(outs),
        out_shape=outs,
        scratch_shapes=[
            pltpu.VMEM((count, keys, 2 * HD), jnp.bfloat16),
            pltpu.VMEM((keys, 2 * HD), jnp.bfloat16),
        ],
        compiler_params=pltpu.CompilerParams(vmem_limit_bytes=26 << 20),
        cost_estimate=pl.CostEstimate(
            flops=4 * WIDE * count * keys * HD, bytes_accessed=count << 20, transcendentals=WIDE * count * keys
        ),
        name="attend_last" if last else "attend_first",
    )(offsets, length, *q, *pieces, *carry)


def column_blocks(zbits):
    return [(yb, zb) for zb in zbits for yb in range(4)]


def body(
    queries, response_keys, response_values, prompt_keys, prompt_values, block_offsets, lengths
):
    mine = split_kv(response_keys[0], response_values[0], prompt_keys, prompt_values)
    q_mine = split_q(queries[0])
    kv = [mine[0]] + [send(mine[bits], Y_STEPS[bits - 1]) for bits in (1, 2, 3)]
    kv, q_mine = lax.optimization_barrier((kv, q_mine))
    column = join(*(part[:TOK] for part in kv))
    prompt = join(*(part[TOK : TOK + 2] for part in kv))
    z_first = send(column, Z_STEPS[0])
    z_second = send(column, Z_STEPS[1])
    for pairs in (CORE_STEP, X_STEPS[0], X_STEPS[1]):
        prompt = double(prompt, pairs)
    q = [q_mine[0]] + [send(q_mine[bits], Y_STEPS[bits - 1]) for bits in (1, 2, 3)]
    z_first, z_second, prompt = lax.optimization_barrier((z_first, z_second, prompt))
    z_both = send(z_first, Z_STEPS[1])
    prompt = double(prompt, ZH_STEP)
    prompts = [send(prompt, pairs) for pairs in Z_STEPS]
    out = attend(block_offsets, lengths, [0, 1, 2, 3], q, [column, z_first, z_second], column_blocks((0, 1, 2)))
    state = {i: (out[i], out[4 + i]) for i in range(4)}
    pieces = [z_both, prompt] + prompts
    blocks = column_blocks((3,)) + [None] * 4
    results = [None] * 4
    for group in GROUPS:
        carry = [state[i][0] for i in group] + [state[i][1] for i in group]
        out = attend(block_offsets, lengths, group, [q[i] for i in group], pieces, blocks, carry, True)
        for i, value in zip(group, out):
            results[i] = send(value, Y_STEPS[i - 1]) if i else value
    return merge(results)[None]


def solution(mesh):
    return jax.shard_map(
        body,
        mesh=mesh,
        in_specs=(
            P("member", "ctx", None),
            P("member", "ctx", None),
            P("member", "ctx", None),
            P(("member", "ctx"), None),
            P(("member", "ctx"), None),
            P("member", None),
            P("member"),
        ),
        out_specs=P("member", "ctx", None),
        check_vma=False,
    )
```

```python
import math

import jax
import jax.numpy as jnp
from jax import lax
from jax.experimental import pallas as pl
from jax.experimental.pallas import tpu as pltpu
from jax.sharding import PartitionSpec as P

HD = 128
KV_HEADS = 4
GROUP = 8
WIDE = GROUP * HD
TOK = 128
RIDE = 16
PAIR = 2
PAIRS = GROUP // PAIR
SCALE = math.log2(math.e) / math.sqrt(HD)
NEG = -1e30
AXES = ("member", "ctx")
VMEM = pl.BlockSpec(memory_space=pltpu.VMEM)
SMEM = pl.BlockSpec(memory_space=pltpu.SMEM)
HBM = pl.BlockSpec(memory_space=pltpu.HBM)


def moves(step):
    pairs = []
    for i in range(256):
        zh, x, c, y, z = i // 128, i // 32 % 4, i // 16 % 2, i // 4 % 4, i % 4
        zh2, x2, c2, y2, z2 = step(zh, x, c, y, z)
        pairs.append((i, (((zh2 * 4 + x2) * 2 + c2) * 4 + y2) * 4 + z2))
    return pairs


Z_STEPS = [moves(lambda zh, x, c, y, z, k=k: (zh, x, c, y, z ^ (1, 2)[c ^ k])) for k in (0, 1)]
Z_STEPS.append(moves(lambda zh, x, c, y, z: (zh, x, c, y, z ^ 3)))
Y_STEPS = [moves(lambda zh, x, c, y, z, k=k: (zh, x, c, y ^ (1, 3)[c ^ k], z)) for k in (0, 1)]
Y_STEPS.append(moves(lambda zh, x, c, y, z: (zh, x, c, y ^ 2, z)))
X_STEPS = [moves(lambda zh, x, c, y, z, k=k: (zh, x ^ (1, 3)[c ^ k], c, y, z)) for k in (0, 1)]
X_STEPS.append(moves(lambda zh, x, c, y, z: (zh, x ^ 2, c, y, z)))
ZH_STEP = moves(lambda zh, x, c, y, z: (zh ^ 1, x, c, y, z))
CORE_STEP = moves(lambda zh, x, c, y, z: (zh, x, c ^ 1, y, z))


def send(value, pairs):
    return lax.ppermute(value, AXES, pairs)


def join(*values):
    return jnp.concatenate(values, axis=0)


def double(value, pairs):
    return join(value, send(value, pairs))


def place():
    ctx, member = lax.axis_index("ctx"), lax.axis_index("member")
    return member % 2, ctx // 4, ctx % 4


def delta(bits, core, first, second):
    step0 = first + core * (second - first)
    step1 = second + core * (first - second)
    return (step0 if bits & 1 else 0) ^ (step1 if bits & 2 else 0)


def head_of(bits):
    core, y, _ = place()
    return y ^ delta(bits, core, 1, 3)


def columns(head, width):
    return pl.ds(pl.multiple_of(head * width, width), width)


def two_rows(pair):
    row = lax.broadcasted_iota(jnp.int32, (RIDE, HD), 0)
    wide = pair.astype(jnp.float32)
    return jnp.where(row == 0, wide[:1], jnp.where(row == 1, wide[1:], 0.0)).astype(jnp.bfloat16)


def run(copies):
    for copy in copies:
        copy.start()
    for copy in copies:
        copy.wait()


def split_kv_kernel(k_ref, v_ref, pk_ref, pv_ref, *refs):
    outs, rows, sems = refs[:4], refs[4], refs[5]
    copies = [
        pltpu.make_async_copy(pk_ref, rows.at[0], sems.at[8]),
        pltpu.make_async_copy(pv_ref, rows.at[1], sems.at[9]),
    ]
    for bits in range(4):
        part = columns(head_of(bits), HD)
        copies.append(pltpu.make_async_copy(k_ref.at[:, part], outs[bits].at[:TOK, :HD], sems.at[bits]))
        copies.append(pltpu.make_async_copy(v_ref.at[:, part], outs[bits].at[:TOK, HD:], sems.at[4 + bits]))
    run(copies)
    for bits in range(4):
        part = columns(head_of(bits), HD)
        outs[bits][TOK:, :HD] = two_rows(rows[0, :, part])
        outs[bits][TOK:, HD:] = two_rows(rows[1, :, part])


def split_kv(keys, values, prompt_keys, prompt_values):
    return pl.pallas_call(
        split_kv_kernel,
        in_specs=[HBM] * 4,
        out_specs=[VMEM] * 4,
        out_shape=[jax.ShapeDtypeStruct((TOK + RIDE, 2 * HD), jnp.bfloat16)] * 4,
        scratch_shapes=[pltpu.VMEM((2, 2, KV_HEADS * HD), jnp.bfloat16), pltpu.SemaphoreType.DMA((10,))],
        name="split_kv",
    )(keys, values, prompt_keys, prompt_values)


def split_q_kernel(q_ref, *refs):
    outs, sems = refs[:4], refs[4]
    run(
        [
            pltpu.make_async_copy(q_ref.at[:, columns(head_of(bits), WIDE)], outs[bits], sems.at[bits])
            for bits in range(4)
        ]
    )


def split_q(q):
    return pl.pallas_call(
        split_q_kernel,
        in_specs=[HBM],
        out_specs=[VMEM] * 4,
        out_shape=[jax.ShapeDtypeStruct((TOK, WIDE), jnp.bfloat16)] * 4,
        scratch_shapes=[pltpu.SemaphoreType.DMA((4,))],
        name="split_q",
    )(q)


def place_kernel(offsets, length, info_ref):
    core, y, z = place()
    row = lax.broadcasted_iota(jnp.int32, info_ref.shape, 0)
    info = jnp.where(row == 16, length[0], 0)
    for zbits in range(4):
        for ybits in range(4):
            source = (y ^ delta(ybits, core, 1, 3)) * 4 + (z ^ delta(zbits, core, 1, 2))
            info = jnp.where(row == zbits * 4 + ybits, offsets[0, source] * TOK, info)
    info_ref[...] = info


def places(offsets, length):
    return pl.pallas_call(
        place_kernel,
        in_specs=[SMEM, SMEM],
        out_specs=VMEM,
        out_shape=jax.ShapeDtypeStruct((24, HD), jnp.int32),
        compiler_params=pltpu.CompilerParams(vmem_limit_bytes=4 << 20),
        name="places",
    )(offsets, length)


def stack_kernel(*refs):
    parts, column_ref, sems = refs[:4], refs[4], refs[5]
    run(
        [
            pltpu.make_async_copy(parts[i].at[:TOK], column_ref.at[i * TOK : (i + 1) * TOK], sems.at[i])
            for i in range(4)
        ]
    )


def stack(parts):
    return pl.pallas_call(
        stack_kernel,
        in_specs=[pl.BlockSpec(memory_space=pl.ANY)] * 4,
        out_specs=VMEM,
        out_shape=jax.ShapeDtypeStruct((4 * TOK, 2 * HD), jnp.bfloat16),
        scratch_shapes=[pltpu.SemaphoreType.DMA((4,))],
        compiler_params=pltpu.CompilerParams(vmem_limit_bytes=4 << 20),
        name="stack",
    )(*parts)


def merge_kernel(*refs):
    parts, out_ref, sems = refs[:4], refs[4], refs[5]
    run(
        [
            pltpu.make_async_copy(parts[bits], out_ref.at[:, columns(head_of(bits), WIDE)], sems.at[bits])
            for bits in range(4)
        ]
    )


def merge(parts):
    return pl.pallas_call(
        merge_kernel,
        in_specs=[VMEM] * 4,
        out_specs=pl.BlockSpec(memory_space=pl.ANY),
        out_shape=jax.ShapeDtypeStruct((TOK, KV_HEADS * WIDE), jnp.bfloat16),
        scratch_shapes=[pltpu.SemaphoreType.DMA((4,))],
        compiler_params=pltpu.CompilerParams(vmem_limit_bytes=8 << 20),
        name="merge",
    )(*parts)


def make_kernel(queries, sizes, blocks, carried, last):
    keys = TOK * len(blocks)
    count = len(queries)

    def kernel(info_ref, *refs):
        q_refs, refs = refs[:count], refs[count:]
        pieces, refs = refs[: len(sizes)], refs[len(sizes) :]
        if carried:
            stat_in, sum_in, refs = refs[:count], refs[count : 2 * count], refs[2 * count :]
        if last:
            outs, refs = refs[:count], refs[count:]
        else:
            stat_out, sum_out, mark_ref = refs[:count], refs[count : 2 * count], refs[2 * count]
            refs = refs[2 * count + 1 :]
            mark_ref[...] = jnp.zeros(mark_ref.shape, jnp.float32)
        k_aug, v_aug = refs
        token = lax.broadcasted_iota(jnp.int32, (TOK, TOK), 1)
        k_row = lax.broadcasted_iota(jnp.int32, (TOK, TOK), 0)

        def first_position(ybits, zbits):
            return info_ref[zbits * 4 + ybits : zbits * 4 + ybits + 1, :]

        for index, bits in enumerate(blocks):
            to = slice(index * TOK, (index + 1) * TOK)
            if bits is not None:
                k_pos = k_row + first_position(bits[0], bits[1])
            for i in range(count):
                if bits is None:
                    bias = jnp.zeros((TOK, TOK), jnp.bfloat16)
                else:
                    q_pos = token + first_position(queries[i], 0)
                    counted = (k_pos <= q_pos) & (k_pos < info_ref[16:17, :])
                    bias = jnp.where(counted, 0.0, NEG).astype(jnp.bfloat16)
                k_aug[i, to, HD:] = bias
        v_aug[:, HD:] = jnp.ones((keys, HD), jnp.bfloat16)
        start = 0
        for piece, size in zip(pieces, sizes):
            v_aug[start : start + size, :HD] = piece[:, HD:]
            for i in range(count):
                k_aug[i, start : start + size, :HD] = piece[:, :HD]
            start += size
        eye = jnp.where(token == k_row, 1.0, 0.0).astype(jnp.bfloat16)
        low = lax.broadcasted_iota(jnp.int32, (1, HD), 1) < HD // 2

        def score(i, h):
            heads = [
                jnp.concatenate([q_refs[i][:, (h * PAIR + u) * HD : (h * PAIR + u + 1) * HD], eye], axis=1)
                for u in range(PAIR)
            ]
            return lax.dot_general(
                jnp.concatenate(heads, axis=0),
                k_aug[i],
                (((1,), (1,)), ((), ())),
                preferred_element_type=jnp.float32,
            )

        def finish(i, h, s):
            top = jnp.max(s, axis=1, keepdims=True)
            if carried:
                stat = stat_in[i][h]
                before = jnp.max(jnp.where(low, stat, -3e38), axis=1, keepdims=True)
                total = jnp.max(jnp.where(low, -3e38, stat), axis=1, keepdims=True)
                top = jnp.maximum(before, top)
                rescale = jnp.exp2((before - top) * SCALE)
            weights = jnp.exp2(s * SCALE - top * SCALE).astype(jnp.bfloat16)
            both = lax.dot_general(
                weights, v_aug[...], (((1,), (0,)), ((), ())), preferred_element_type=jnp.float32
            )
            weighted, totals = both[:, :HD], both[:, HD:]
            if carried:
                weighted = weighted + sum_in[i][h] * rescale
                totals = totals + total * rescale
            if last:
                result = (weighted / totals).astype(jnp.bfloat16)
                for u in range(PAIR):
                    outs[i][:, (h * PAIR + u) * HD : (h * PAIR + u + 1) * HD] = result[u * TOK : (u + 1) * TOK]
            else:
                stat_out[i][h] = jnp.where(low, top, totals)
                sum_out[i][h] = weighted

        steps = [(i, h) for i in range(count) for h in range(PAIRS)]
        s = score(*steps[0])
        for n, step in enumerate(steps):
            ahead = score(*steps[n + 1]) if n + 1 < len(steps) else None
            finish(*step, s)
            s = ahead

    return kernel


def attend(info, queries, q, pieces, blocks, carry=(), last=False):
    sizes = [p.shape[0] for p in pieces]
    keys, count = TOK * len(blocks), len(queries)
    state = jax.ShapeDtypeStruct((PAIRS, PAIR * TOK, HD), jnp.float32)
    result = jax.ShapeDtypeStruct((TOK, WIDE), jnp.bfloat16)
    mark = jax.ShapeDtypeStruct((8, HD), jnp.float32)
    outs = [result] * count if last else [state] * (2 * count) + [mark]
    return pl.pallas_call(
        make_kernel(queries, sizes, blocks, bool(carry), last),
        in_specs=[VMEM] * (1 + count + len(pieces) + len(carry)),
        out_specs=[VMEM] * len(outs),
        out_shape=outs,
        scratch_shapes=[
            pltpu.VMEM((count, keys, 2 * HD), jnp.bfloat16),
            pltpu.VMEM((keys, 2 * HD), jnp.bfloat16),
        ],
        compiler_params=pltpu.CompilerParams(vmem_limit_bytes=26 << 20),
        cost_estimate=pl.CostEstimate(
            flops=4 * WIDE * count * keys * HD, bytes_accessed=count << 20, transcendentals=WIDE * count * keys
        ),
        name="attend_last" if last else "attend_first",
    )(info, *q, *pieces, *carry)


def column_blocks(zbits):
    return [(yb, zb) for zb in zbits for yb in range(4)]


def body(
    queries, response_keys, response_values, prompt_keys, prompt_values, block_offsets, lengths
):
    mine = split_kv(response_keys[0], response_values[0], prompt_keys, prompt_values)
    queries, mine = lax.optimization_barrier((queries, mine))
    q_mine = split_q(queries[0])
    kv = [mine[0]] + [send(mine[bits], Y_STEPS[bits - 1]) for bits in (1, 2, 3)]
    column = stack(kv)
    prompt = join(*(part[TOK : TOK + 2] for part in kv))
    z_first = send(column, Z_STEPS[0])
    z_second = send(column, Z_STEPS[1])
    column, q_mine = lax.optimization_barrier((column, q_mine))
    q = [q_mine[0]] + [send(q_mine[bits], Y_STEPS[bits - 1]) for bits in (1, 2, 3)]
    prompt = double(prompt, CORE_STEP)
    prompt = double(prompt, X_STEPS[0])
    block_offsets, prompt = lax.optimization_barrier((block_offsets, prompt))
    info = places(block_offsets, lengths)
    q[1], prompt = lax.optimization_barrier((q[1], prompt))
    prompt = double(prompt, X_STEPS[1])
    z_first, z_second, prompt = lax.optimization_barrier((z_first, z_second, prompt))
    z_both = send(z_first, Z_STEPS[1])
    prompt = double(prompt, ZH_STEP)
    near = [column, z_first, z_second]

    def begin(group):
        out = attend(info, group, [q[i] for i in group], near, column_blocks((0, 1, 2)))
        return {i: [out[n], out[len(group) + n]] for n, i in enumerate(group)}, out[-1]

    state, mark = begin([3, 1])
    mark, prompt = lax.optimization_barrier((mark, prompt))
    prompts = [send(prompt, pairs) for pairs in Z_STEPS]
    state |= begin([2])[0]
    pieces = [z_both, prompt] + prompts
    late = column_blocks((3,)) + [None] * 4
    results = [None] * 4
    for i in (3, 1, 2, 0):
        if i in state:
            out = attend(info, [i], [q[i]], pieces, late, state[i], True)[0]
        else:
            out = attend(
                info, [i], [q[i]], near + pieces, column_blocks((0, 1, 2)) + late, (), True
            )[0]
        results[i] = send(out, Y_STEPS[i - 1]) if i else out
    return merge(results)[None]


def solution(mesh):
    return jax.shard_map(
        body,
        mesh=mesh,
        in_specs=(
            P("member", "ctx", None),
            P("member", "ctx", None),
            P("member", "ctx", None),
            P(("member", "ctx"), None),
            P(("member", "ctx"), None),
            P("member", None),
            P("member"),
        ),
        out_specs=P("member", "ctx", None),
        check_vma=False,
    )
```

```python
import math

import jax
import jax.numpy as jnp
from jax import lax
from jax.experimental import pallas as pl
from jax.experimental.pallas import tpu as pltpu
from jax.sharding import PartitionSpec as P

HD = 128
KV_HEADS = 4
GROUP = 8
WIDE = GROUP * HD
TOK = 128
RIDE = 16
PAIR = 4
PAIRS = GROUP // PAIR
SCALE = math.log2(math.e) / math.sqrt(HD)
NEG = -1e30
AXES = ("member", "ctx")
VMEM = pl.BlockSpec(memory_space=pltpu.VMEM)
SMEM = pl.BlockSpec(memory_space=pltpu.SMEM)
HBM = pl.BlockSpec(memory_space=pltpu.HBM)


def moves(step):
    pairs = []
    for i in range(256):
        zh, x, c, y, z = i // 128, i // 32 % 4, i // 16 % 2, i // 4 % 4, i % 4
        zh2, x2, c2, y2, z2 = step(zh, x, c, y, z)
        pairs.append((i, (((zh2 * 4 + x2) * 2 + c2) * 4 + y2) * 4 + z2))
    return pairs


Z_STEPS = [moves(lambda zh, x, c, y, z, k=k: (zh, x, c, y, z ^ (1, 2)[c ^ k])) for k in (0, 1)]
Z_STEPS.append(moves(lambda zh, x, c, y, z: (zh, x, c, y, z ^ 3)))
Y_STEPS = [moves(lambda zh, x, c, y, z, k=k: (zh, x, c, y ^ (1, 3)[c ^ k], z)) for k in (0, 1)]
Y_STEPS.append(moves(lambda zh, x, c, y, z: (zh, x, c, y ^ 2, z)))
X_STEPS = [moves(lambda zh, x, c, y, z, k=k: (zh, x ^ (1, 3)[c ^ k], c, y, z)) for k in (0, 1)]
X_STEPS.append(moves(lambda zh, x, c, y, z: (zh, x ^ 2, c, y, z)))
ZH_STEP = moves(lambda zh, x, c, y, z: (zh ^ 1, x, c, y, z))
CORE_STEP = moves(lambda zh, x, c, y, z: (zh, x, c ^ 1, y, z))


def send(value, pairs):
    return lax.ppermute(value, AXES, pairs)


def join(*values):
    return jnp.concatenate(values, axis=0)


def double(value, pairs):
    return join(value, send(value, pairs))


def place():
    ctx, member = lax.axis_index("ctx"), lax.axis_index("member")
    return member % 2, ctx // 4, ctx % 4


def delta(bits, core, first, second):
    step0 = first + core * (second - first)
    step1 = second + core * (first - second)
    return (step0 if bits & 1 else 0) ^ (step1 if bits & 2 else 0)


def head_of(bits):
    core, y, _ = place()
    return y ^ delta(bits, core, 1, 3)


def columns(head, width):
    return pl.ds(pl.multiple_of(head * width, width), width)


def two_rows(pair):
    row = lax.broadcasted_iota(jnp.int32, (RIDE, HD), 0)
    wide = pair.astype(jnp.float32)
    return jnp.where(row == 0, wide[:1], jnp.where(row == 1, wide[1:], 0.0)).astype(jnp.bfloat16)


def run(copies):
    for copy in copies:
        copy.start()
    for copy in copies:
        copy.wait()


def split_kv_kernel(k_ref, v_ref, pk_ref, pv_ref, *refs):
    outs, rows, sems = refs[:4], refs[4], refs[5]
    copies = [
        pltpu.make_async_copy(pk_ref, rows.at[0], sems.at[8]),
        pltpu.make_async_copy(pv_ref, rows.at[1], sems.at[9]),
    ]
    for bits in range(4):
        part = columns(head_of(bits), HD)
        copies.append(pltpu.make_async_copy(k_ref.at[:, part], outs[bits].at[:TOK, :HD], sems.at[bits]))
        copies.append(pltpu.make_async_copy(v_ref.at[:, part], outs[bits].at[:TOK, HD:], sems.at[4 + bits]))
    run(copies)
    for bits in range(4):
        part = columns(head_of(bits), HD)
        outs[bits][TOK:, :HD] = two_rows(rows[0, :, part])
        outs[bits][TOK:, HD:] = two_rows(rows[1, :, part])


def split_kv(keys, values, prompt_keys, prompt_values):
    return pl.pallas_call(
        split_kv_kernel,
        in_specs=[HBM] * 4,
        out_specs=[VMEM] * 4,
        out_shape=[pltpu.VMEM((TOK + RIDE, 2 * HD), jnp.bfloat16)] * 4,
        scratch_shapes=[pltpu.VMEM((2, 2, KV_HEADS * HD), jnp.bfloat16), pltpu.SemaphoreType.DMA((10,))],
        name="split_kv",
    )(keys, values, prompt_keys, prompt_values)


def split_q_kernel(q_ref, *refs):
    outs, sems = refs[:4], refs[4]
    run(
        [
            pltpu.make_async_copy(q_ref.at[:, columns(head_of(bits), WIDE)], outs[bits], sems.at[bits])
            for bits in range(4)
        ]
    )


def split_q(q):
    return pl.pallas_call(
        split_q_kernel,
        in_specs=[HBM],
        out_specs=[VMEM] * 4,
        out_shape=[pltpu.VMEM((TOK, WIDE), jnp.bfloat16)] * 4,
        scratch_shapes=[pltpu.SemaphoreType.DMA((4,))],
        name="split_q",
    )(q)


def place_kernel(offsets, length, info_ref):
    core, y, z = place()
    row = lax.broadcasted_iota(jnp.int32, info_ref.shape, 0)
    info = jnp.where(row == 16, length[0], 0)
    for zbits in range(4):
        for ybits in range(4):
            source = (y ^ delta(ybits, core, 1, 3)) * 4 + (z ^ delta(zbits, core, 1, 2))
            info = jnp.where(row == zbits * 4 + ybits, offsets[0, source] * TOK, info)
    info_ref[...] = info


def places(offsets, length):
    return pl.pallas_call(
        place_kernel,
        in_specs=[SMEM, SMEM],
        out_specs=VMEM,
        out_shape=jax.ShapeDtypeStruct((24, HD), jnp.int32),
        compiler_params=pltpu.CompilerParams(vmem_limit_bytes=4 << 20),
        name="places",
    )(offsets, length)


def stack_kernel(*refs):
    parts, column_ref, sems = refs[:4], refs[4], refs[5]
    run(
        [
            pltpu.make_async_copy(parts[i].at[:TOK], column_ref.at[i * TOK : (i + 1) * TOK], sems.at[i])
            for i in range(4)
        ]
    )


def stack(parts):
    return pl.pallas_call(
        stack_kernel,
        in_specs=[pl.BlockSpec(memory_space=pl.ANY)] * 4,
        out_specs=VMEM,
        out_shape=jax.ShapeDtypeStruct((4 * TOK, 2 * HD), jnp.bfloat16),
        scratch_shapes=[pltpu.SemaphoreType.DMA((4,))],
        compiler_params=pltpu.CompilerParams(vmem_limit_bytes=4 << 20),
        name="stack",
    )(*parts)


def merge_kernel(*refs):
    parts, out_ref, sems = refs[:4], refs[4], refs[5]
    run(
        [
            pltpu.make_async_copy(parts[bits], out_ref.at[:, columns(head_of(bits), WIDE)], sems.at[bits])
            for bits in range(4)
        ]
    )


def merge(parts):
    return pl.pallas_call(
        merge_kernel,
        in_specs=[VMEM] * 4,
        out_specs=pl.BlockSpec(memory_space=pl.ANY),
        out_shape=jax.ShapeDtypeStruct((TOK, KV_HEADS * WIDE), jnp.bfloat16),
        scratch_shapes=[pltpu.SemaphoreType.DMA((4,))],
        compiler_params=pltpu.CompilerParams(vmem_limit_bytes=8 << 20),
        name="merge",
    )(*parts)


def make_kernel(queries, sizes, blocks, carried, last):
    keys = TOK * len(blocks)
    count = len(queries)

    def kernel(info_ref, *refs):
        q_refs, refs = refs[:count], refs[count:]
        pieces, refs = refs[: len(sizes)], refs[len(sizes) :]
        if carried:
            stat_in, sum_in, refs = refs[:count], refs[count : 2 * count], refs[2 * count :]
        if last:
            outs, refs = refs[:count], refs[count:]
        else:
            stat_out, sum_out, mark_ref = refs[:count], refs[count : 2 * count], refs[2 * count]
            refs = refs[2 * count + 1 :]
            mark_ref[...] = jnp.zeros(mark_ref.shape, jnp.float32)
        k_aug, v_aug = refs
        token = lax.broadcasted_iota(jnp.int32, (TOK, TOK), 1)
        k_row = lax.broadcasted_iota(jnp.int32, (TOK, TOK), 0)

        def first_position(ybits, zbits):
            return info_ref[zbits * 4 + ybits : zbits * 4 + ybits + 1, :]

        for index, bits in enumerate(blocks):
            to = slice(index * TOK, (index + 1) * TOK)
            if bits is not None:
                k_pos = k_row + first_position(bits[0], bits[1])
            for i in range(count):
                if bits is None:
                    bias = jnp.zeros((TOK, TOK), jnp.bfloat16)
                else:
                    q_pos = token + first_position(queries[i], 0)
                    counted = (k_pos <= q_pos) & (k_pos < info_ref[16:17, :])
                    bias = jnp.where(counted, 0.0, NEG).astype(jnp.bfloat16)
                k_aug[i, to, HD:] = bias
        v_aug[:, HD:] = jnp.ones((keys, HD), jnp.bfloat16)
        start = 0
        for piece, size in zip(pieces, sizes):
            v_aug[start : start + size, :HD] = piece[:, HD:]
            for i in range(count):
                k_aug[i, start : start + size, :HD] = piece[:, :HD]
            start += size
        eye = jnp.where(token == k_row, 1.0, 0.0).astype(jnp.bfloat16)
        low = lax.broadcasted_iota(jnp.int32, (1, HD), 1) < HD // 2

        def score(i, h):
            heads = [
                jnp.concatenate([q_refs[i][:, (h * PAIR + u) * HD : (h * PAIR + u + 1) * HD], eye], axis=1)
                for u in range(PAIR)
            ]
            return lax.dot_general(
                jnp.concatenate(heads, axis=0),
                k_aug[i],
                (((1,), (1,)), ((), ())),
                preferred_element_type=jnp.float32,
            )

        def finish(i, h, s):
            top = jnp.max(s, axis=1, keepdims=True)
            if carried:
                stat = stat_in[i][h]
                before = jnp.max(jnp.where(low, stat, -3e38), axis=1, keepdims=True)
                total = jnp.max(jnp.where(low, -3e38, stat), axis=1, keepdims=True)
                top = jnp.maximum(before, top)
                rescale = jnp.exp2((before - top) * SCALE)
            weights = jnp.exp2(s * SCALE - top * SCALE).astype(jnp.bfloat16)
            both = lax.dot_general(
                weights, v_aug[...], (((1,), (0,)), ((), ())), preferred_element_type=jnp.float32
            )
            weighted, totals = both[:, :HD], both[:, HD:]
            if carried:
                weighted = weighted + sum_in[i][h] * rescale
                totals = totals + total * rescale
            if last:
                result = (weighted / totals).astype(jnp.bfloat16)
                for u in range(PAIR):
                    outs[i][:, (h * PAIR + u) * HD : (h * PAIR + u + 1) * HD] = result[u * TOK : (u + 1) * TOK]
            else:
                stat_out[i][h] = jnp.where(low, top, totals)
                sum_out[i][h] = weighted

        steps = [(i, h) for i in range(count) for h in range(PAIRS)]
        s = score(*steps[0])
        for n, step in enumerate(steps):
            ahead = score(*steps[n + 1]) if n + 1 < len(steps) else None
            finish(*step, s)
            s = ahead

    return kernel


def attend(info, queries, q, pieces, blocks, carry=(), last=False):
    sizes = [p.shape[0] for p in pieces]
    keys, count = TOK * len(blocks), len(queries)
    state = jax.ShapeDtypeStruct((PAIRS, PAIR * TOK, HD), jnp.float32)
    result = jax.ShapeDtypeStruct((TOK, WIDE), jnp.bfloat16)
    mark = jax.ShapeDtypeStruct((8, HD), jnp.float32)
    outs = [result] * count if last else [state] * (2 * count) + [mark]
    return pl.pallas_call(
        make_kernel(queries, sizes, blocks, bool(carry), last),
        in_specs=[VMEM] * (1 + count + len(pieces) + len(carry)),
        out_specs=[VMEM] * len(outs),
        out_shape=outs,
        scratch_shapes=[
            pltpu.VMEM((count, keys, 2 * HD), jnp.bfloat16),
            pltpu.VMEM((keys, 2 * HD), jnp.bfloat16),
        ],
        compiler_params=pltpu.CompilerParams(vmem_limit_bytes=26 << 20),
        cost_estimate=pl.CostEstimate(
            flops=4 * WIDE * count * keys * HD, bytes_accessed=count << 20, transcendentals=WIDE * count * keys
        ),
        name="attend_last" if last else "attend_first",
    )(info, *q, *pieces, *carry)


def column_blocks(zbits):
    return [(yb, zb) for zb in zbits for yb in range(4)]


def body(
    queries, response_keys, response_values, prompt_keys, prompt_values, block_offsets, lengths
):
    mine = split_kv(response_keys[0], response_values[0], prompt_keys, prompt_values)
    queries, mine = lax.optimization_barrier((queries, mine))
    q_mine = split_q(queries[0])
    kv = [mine[0]] + [send(mine[bits], Y_STEPS[bits - 1]) for bits in (1, 2, 3)]
    column = stack(kv)
    prompt = join(*(part[TOK : TOK + 2] for part in kv))
    z_first = send(column, Z_STEPS[0])
    z_second = send(column, Z_STEPS[1])
    column, q_mine = lax.optimization_barrier((column, q_mine))
    q = [q_mine[0]] + [send(q_mine[bits], Y_STEPS[bits - 1]) for bits in (1, 2, 3)]
    prompt = double(prompt, CORE_STEP)
    prompt = double(prompt, X_STEPS[0])
    block_offsets, prompt = lax.optimization_barrier((block_offsets, prompt))
    info = places(block_offsets, lengths)
    q[1], prompt = lax.optimization_barrier((q[1], prompt))
    prompt = double(prompt, X_STEPS[1])
    z_first, z_second, prompt = lax.optimization_barrier((z_first, z_second, prompt))
    z_both = send(z_first, Z_STEPS[1])
    prompt = double(prompt, ZH_STEP)
    near = [column, z_first, z_second]

    def begin(group):
        out = attend(info, group, [q[i] for i in group], near, column_blocks((0, 1, 2)))
        return {i: [out[n], out[len(group) + n]] for n, i in enumerate(group)}, out[-1]

    state, mark = begin([1, 2])
    mark, prompt = lax.optimization_barrier((mark, prompt))
    prompts = [send(prompt, pairs) for pairs in Z_STEPS]
    state |= begin([3])[0]
    pieces = [z_both, prompt] + prompts
    late = column_blocks((3,)) + [None] * 4
    results = [None] * 4
    for i in (3, 1, 2, 0):
        if i in state:
            out = attend(info, [i], [q[i]], pieces, late, state[i], True)[0]
        else:
            out = attend(
                info, [i], [q[i]], near + pieces, column_blocks((0, 1, 2)) + late, (), True
            )[0]
        results[i] = send(out, Y_STEPS[i - 1]) if i else out
    return merge(results)[None]


def solution(mesh):
    return jax.shard_map(
        body,
        mesh=mesh,
        in_specs=(
            P("member", "ctx", None),
            P("member", "ctx", None),
            P("member", "ctx", None),
            P(("member", "ctx"), None),
            P(("member", "ctx"), None),
            P("member", None),
            P("member"),
        ),
        out_specs=P("member", "ctx", None),
        check_vma=False,
    )
```

```python
import math

import jax
import jax.numpy as jnp
from jax import lax
from jax.experimental import pallas as pl
from jax.experimental.pallas import tpu as pltpu
from jax.sharding import PartitionSpec as P

HD = 128
KV_HEADS = 4
GROUP = 8
WIDE = GROUP * HD
TOK = 128
RIDE = 16
PAIR = 4
PAIRS = GROUP // PAIR
SCALE = math.log2(math.e) / math.sqrt(HD)
NEG = -1e30
AXES = ("member", "ctx")
VMEM = pl.BlockSpec(memory_space=pltpu.VMEM)
SMEM = pl.BlockSpec(memory_space=pltpu.SMEM)
HBM = pl.BlockSpec(memory_space=pltpu.HBM)


def moves(step):
    pairs = []
    for i in range(256):
        zh, x, c, y, z = i // 128, i // 32 % 4, i // 16 % 2, i // 4 % 4, i % 4
        zh2, x2, c2, y2, z2 = step(zh, x, c, y, z)
        pairs.append((i, (((zh2 * 4 + x2) * 2 + c2) * 4 + y2) * 4 + z2))
    return pairs


Z_STEPS = [moves(lambda zh, x, c, y, z, k=k: (zh, x, c, y, z ^ (1, 2)[c ^ k])) for k in (0, 1)]
Z_STEPS.append(moves(lambda zh, x, c, y, z: (zh, x, c, y, z ^ 3)))
Y_STEPS = [moves(lambda zh, x, c, y, z, k=k: (zh, x, c, y ^ (1, 3)[c ^ k], z)) for k in (0, 1)]
Y_STEPS.append(moves(lambda zh, x, c, y, z: (zh, x, c, y ^ 2, z)))
X_STEPS = [moves(lambda zh, x, c, y, z, k=k: (zh, x ^ (1, 3)[c ^ k], c, y, z)) for k in (0, 1)]
X_STEPS.append(moves(lambda zh, x, c, y, z: (zh, x ^ 2, c, y, z)))
ZH_STEP = moves(lambda zh, x, c, y, z: (zh ^ 1, x, c, y, z))
CORE_STEP = moves(lambda zh, x, c, y, z: (zh, x, c ^ 1, y, z))


def send(value, pairs):
    return lax.ppermute(value, AXES, pairs)


def join(*values):
    return jnp.concatenate(values, axis=0)


def double(value, pairs):
    return join(value, send(value, pairs))


def place():
    ctx, member = lax.axis_index("ctx"), lax.axis_index("member")
    return member % 2, ctx // 4, ctx % 4


def delta(bits, core, first, second):
    step0 = first + core * (second - first)
    step1 = second + core * (first - second)
    return (step0 if bits & 1 else 0) ^ (step1 if bits & 2 else 0)


def head_of(bits):
    core, y, _ = place()
    return y ^ delta(bits, core, 1, 3)


def columns(head, width):
    return pl.ds(pl.multiple_of(head * width, width), width)


def two_rows(pair):
    row = lax.broadcasted_iota(jnp.int32, (RIDE, HD), 0)
    wide = pair.astype(jnp.float32)
    return jnp.where(row == 0, wide[:1], jnp.where(row == 1, wide[1:], 0.0)).astype(jnp.bfloat16)


def run(copies):
    for copy in copies:
        copy.start()
    for copy in copies:
        copy.wait()


def split_kv_kernel(k_ref, v_ref, pk_ref, pv_ref, *refs):
    outs, rows, sems = refs[:4], refs[4], refs[5]
    copies = [
        pltpu.make_async_copy(pk_ref, rows.at[0], sems.at[8]),
        pltpu.make_async_copy(pv_ref, rows.at[1], sems.at[9]),
    ]
    for bits in range(4):
        part = columns(head_of(bits), HD)
        copies.append(pltpu.make_async_copy(k_ref.at[:, part], outs[bits].at[:TOK, :HD], sems.at[bits]))
        copies.append(pltpu.make_async_copy(v_ref.at[:, part], outs[bits].at[:TOK, HD:], sems.at[4 + bits]))
    run(copies)
    for bits in range(4):
        part = columns(head_of(bits), HD)
        outs[bits][TOK:, :HD] = two_rows(rows[0, :, part])
        outs[bits][TOK:, HD:] = two_rows(rows[1, :, part])


def split_kv(keys, values, prompt_keys, prompt_values):
    return pl.pallas_call(
        split_kv_kernel,
        in_specs=[HBM] * 4,
        out_specs=[VMEM] * 4,
        out_shape=[pltpu.VMEM((TOK + RIDE, 2 * HD), jnp.bfloat16)] * 4,
        scratch_shapes=[pltpu.VMEM((2, 2, KV_HEADS * HD), jnp.bfloat16), pltpu.SemaphoreType.DMA((10,))],
        name="split_kv",
    )(keys, values, prompt_keys, prompt_values)


def split_q_kernel(q_ref, *refs):
    outs, sems = refs[:4], refs[4]
    run(
        [
            pltpu.make_async_copy(q_ref.at[:, columns(head_of(bits), WIDE)], outs[bits], sems.at[bits])
            for bits in range(4)
        ]
    )


def split_q(q):
    return pl.pallas_call(
        split_q_kernel,
        in_specs=[HBM],
        out_specs=[VMEM] * 4,
        out_shape=[pltpu.VMEM((TOK, WIDE), jnp.bfloat16)] * 4,
        scratch_shapes=[pltpu.SemaphoreType.DMA((4,))],
        name="split_q",
    )(q)


def place_kernel(offsets, length, info_ref):
    core, y, z = place()
    row = lax.broadcasted_iota(jnp.int32, info_ref.shape, 0)
    info = jnp.where(row == 16, length[0], 0)
    for zbits in range(4):
        for ybits in range(4):
            source = (y ^ delta(ybits, core, 1, 3)) * 4 + (z ^ delta(zbits, core, 1, 2))
            info = jnp.where(row == zbits * 4 + ybits, offsets[0, source] * TOK, info)
    info_ref[...] = info


def places(offsets, length):
    return pl.pallas_call(
        place_kernel,
        in_specs=[SMEM, SMEM],
        out_specs=VMEM,
        out_shape=jax.ShapeDtypeStruct((24, HD), jnp.int32),
        compiler_params=pltpu.CompilerParams(vmem_limit_bytes=4 << 20),
        name="places",
    )(offsets, length)


def stack_kernel(*refs):
    parts, column_ref, sems = refs[:4], refs[4], refs[5]
    run(
        [
            pltpu.make_async_copy(parts[i].at[:TOK], column_ref.at[i * TOK : (i + 1) * TOK], sems.at[i])
            for i in range(4)
        ]
    )


def stack(parts):
    return pl.pallas_call(
        stack_kernel,
        in_specs=[pl.BlockSpec(memory_space=pl.ANY)] * 4,
        out_specs=VMEM,
        out_shape=jax.ShapeDtypeStruct((4 * TOK, 2 * HD), jnp.bfloat16),
        scratch_shapes=[pltpu.SemaphoreType.DMA((4,))],
        compiler_params=pltpu.CompilerParams(vmem_limit_bytes=4 << 20),
        name="stack",
    )(*parts)


def merge_kernel(*refs):
    parts, out_ref, sems = refs[:4], refs[4], refs[5]
    run(
        [
            pltpu.make_async_copy(parts[bits], out_ref.at[:, columns(head_of(bits), WIDE)], sems.at[bits])
            for bits in range(4)
        ]
    )


def merge(parts):
    return pl.pallas_call(
        merge_kernel,
        in_specs=[VMEM] * 4,
        out_specs=pl.BlockSpec(memory_space=pl.ANY),
        out_shape=jax.ShapeDtypeStruct((TOK, KV_HEADS * WIDE), jnp.bfloat16),
        scratch_shapes=[pltpu.SemaphoreType.DMA((4,))],
        compiler_params=pltpu.CompilerParams(vmem_limit_bytes=8 << 20),
        name="merge",
    )(*parts)


def make_kernel(queries, sizes, blocks, carried, last):
    keys = TOK * len(blocks)
    count = len(queries)

    def kernel(info_ref, *refs):
        q_refs, refs = refs[:count], refs[count:]
        pieces, refs = refs[: len(sizes)], refs[len(sizes) :]
        if carried:
            stat_in, sum_in, refs = refs[:count], refs[count : 2 * count], refs[2 * count :]
        if last:
            outs, refs = refs[:count], refs[count:]
        else:
            stat_out, sum_out, refs = refs[:count], refs[count : 2 * count], refs[2 * count :]
        k_aug, v_aug = refs
        token = lax.broadcasted_iota(jnp.int32, (TOK, TOK), 1)
        k_row = lax.broadcasted_iota(jnp.int32, (TOK, TOK), 0)

        def first_position(ybits, zbits):
            return info_ref[zbits * 4 + ybits : zbits * 4 + ybits + 1, :]

        for index, bits in enumerate(blocks):
            to = slice(index * TOK, (index + 1) * TOK)
            if bits is not None:
                k_pos = k_row + first_position(bits[0], bits[1])
            for i in range(count):
                if bits is None:
                    bias = jnp.zeros((TOK, TOK), jnp.bfloat16)
                else:
                    q_pos = token + first_position(queries[i], 0)
                    counted = (k_pos <= q_pos) & (k_pos < info_ref[16:17, :])
                    bias = jnp.where(counted, 0.0, NEG).astype(jnp.bfloat16)
                k_aug[i, to, HD:] = bias
        v_aug[:, HD:] = jnp.ones((keys, HD), jnp.bfloat16)
        start = 0
        for piece, size in zip(pieces, sizes):
            v_aug[start : start + size, :HD] = piece[:, HD:]
            for i in range(count):
                k_aug[i, start : start + size, :HD] = piece[:, :HD]
            start += size
        eye = jnp.where(token == k_row, 1.0, 0.0).astype(jnp.bfloat16)
        low = lax.broadcasted_iota(jnp.int32, (1, HD), 1) < HD // 2

        def score(i, h):
            heads = [
                jnp.concatenate([q_refs[i][:, (h * PAIR + u) * HD : (h * PAIR + u + 1) * HD], eye], axis=1)
                for u in range(PAIR)
            ]
            return lax.dot_general(
                jnp.concatenate(heads, axis=0),
                k_aug[i],
                (((1,), (1,)), ((), ())),
                preferred_element_type=jnp.float32,
            )

        def finish(i, h, s):
            top = jnp.max(s, axis=1, keepdims=True)
            if carried:
                stat = stat_in[i][h]
                before = jnp.max(jnp.where(low, stat, -3e38), axis=1, keepdims=True)
                total = jnp.max(jnp.where(low, -3e38, stat), axis=1, keepdims=True)
                top = jnp.maximum(before, top)
                rescale = jnp.exp2((before - top) * SCALE)
            weights = jnp.exp2(s * SCALE - top * SCALE).astype(jnp.bfloat16)
            both = lax.dot_general(
                weights, v_aug[...], (((1,), (0,)), ((), ())), preferred_element_type=jnp.float32
            )
            weighted, totals = both[:, :HD], both[:, HD:]
            if carried:
                weighted = weighted + sum_in[i][h] * rescale
                totals = totals + total * rescale
            if last:
                result = (weighted / totals).astype(jnp.bfloat16)
                for u in range(PAIR):
                    outs[i][:, (h * PAIR + u) * HD : (h * PAIR + u + 1) * HD] = result[u * TOK : (u + 1) * TOK]
            else:
                stat_out[i][h] = jnp.where(low, top, totals)
                sum_out[i][h] = weighted

        steps = [(i, h) for i in range(count) for h in range(PAIRS)]
        s = score(*steps[0])
        for n, step in enumerate(steps):
            ahead = score(*steps[n + 1]) if n + 1 < len(steps) else None
            finish(*step, s)
            s = ahead

    return kernel


def attend(info, queries, q, pieces, blocks, carry=(), last=False):
    sizes = [p.shape[0] for p in pieces]
    keys, count = TOK * len(blocks), len(queries)
    state = jax.ShapeDtypeStruct((PAIRS, PAIR * TOK, HD), jnp.float32)
    result = jax.ShapeDtypeStruct((TOK, WIDE), jnp.bfloat16)
    outs = [result] * count if last else [state] * (2 * count)
    return pl.pallas_call(
        make_kernel(queries, sizes, blocks, bool(carry), last),
        in_specs=[VMEM] * (1 + count + len(pieces) + len(carry)),
        out_specs=[VMEM] * len(outs),
        out_shape=outs,
        scratch_shapes=[
            pltpu.VMEM((count, keys, 2 * HD), jnp.bfloat16),
            pltpu.VMEM((keys, 2 * HD), jnp.bfloat16),
        ],
        compiler_params=pltpu.CompilerParams(vmem_limit_bytes=26 << 20),
        cost_estimate=pl.CostEstimate(
            flops=4 * WIDE * count * keys * HD, bytes_accessed=count << 20, transcendentals=WIDE * count * keys
        ),
        name="attend_last" if last else "attend_first",
    )(info, *q, *pieces, *carry)


def column_blocks(zbits):
    return [(yb, zb) for zb in zbits for yb in range(4)]


def body(
    queries, response_keys, response_values, prompt_keys, prompt_values, block_offsets, lengths
):
    mine = split_kv(response_keys[0], response_values[0], prompt_keys, prompt_values)
    queries, mine = lax.optimization_barrier((queries, mine))
    q_mine = split_q(queries[0])
    kv = [mine[0]] + [send(mine[bits], Y_STEPS[bits - 1]) for bits in (1, 2, 3)]
    column = stack(kv)
    prompt = join(*(part[TOK : TOK + 2] for part in kv))
    z_first = send(column, Z_STEPS[0])
    z_second = send(column, Z_STEPS[1])
    column, q_mine = lax.optimization_barrier((column, q_mine))
    q = [q_mine[0]] + [send(q_mine[bits], Y_STEPS[bits - 1]) for bits in (1, 2, 3)]
    prompt = double(prompt, CORE_STEP)
    prompt = double(prompt, X_STEPS[0])
    block_offsets, prompt = lax.optimization_barrier((block_offsets, prompt))
    info = places(block_offsets, lengths)
    q[1], prompt = lax.optimization_barrier((q[1], prompt))
    prompt = double(prompt, X_STEPS[1])
    z_first, z_second, prompt = lax.optimization_barrier((z_first, z_second, prompt))
    z_both = send(z_first, Z_STEPS[1])
    prompt = double(prompt, ZH_STEP)
    near = [column, z_first, z_second]

    def begin(group):
        out = attend(info, group, [q[i] for i in group], near, column_blocks((0, 1, 2)))
        return {i: [out[n], out[len(group) + n]] for n, i in enumerate(group)}

    state = begin([1, 2])
    prompts = [send(prompt, pairs) for pairs in Z_STEPS]
    state |= begin([3])
    pieces = [z_both, prompt] + prompts
    late = column_blocks((3,)) + [None] * 4
    results = [None] * 4
    for i in (3, 1, 2, 0):
        if i in state:
            out = attend(info, [i], [q[i]], pieces, late, state[i], True)[0]
        else:
            out = attend(
                info, [i], [q[i]], near + pieces, column_blocks((0, 1, 2)) + late, (), True
            )[0]
        results[i] = send(out, Y_STEPS[i - 1]) if i else out
    return merge(results)[None]


def solution(mesh):
    return jax.shard_map(
        body,
        mesh=mesh,
        in_specs=(
            P("member", "ctx", None),
            P("member", "ctx", None),
            P("member", "ctx", None),
            P(("member", "ctx"), None),
            P(("member", "ctx"), None),
            P("member", None),
            P("member"),
        ),
        out_specs=P("member", "ctx", None),
        check_vma=False,
    )
```

```python
import math

import jax
import jax.numpy as jnp
from jax import lax
from jax.experimental import pallas as pl
from jax.experimental.pallas import tpu as pltpu
from jax.sharding import PartitionSpec as P

HD = 128
KV_HEADS = 4
GROUP = 8
WIDE = GROUP * HD
TOK = 128
RIDE = 16
PAIR = 4
PAIRS = GROUP // PAIR
SCALE = math.log2(math.e) / math.sqrt(HD)
NEG = -1e30
AXES = ("member", "ctx")
VMEM = pl.BlockSpec(memory_space=pltpu.VMEM)
SMEM = pl.BlockSpec(memory_space=pltpu.SMEM)
HBM = pl.BlockSpec(memory_space=pltpu.HBM)


def moves(step):
    pairs = []
    for i in range(256):
        zh, x, c, y, z = i // 128, i // 32 % 4, i // 16 % 2, i // 4 % 4, i % 4
        zh2, x2, c2, y2, z2 = step(zh, x, c, y, z)
        pairs.append((i, (((zh2 * 4 + x2) * 2 + c2) * 4 + y2) * 4 + z2))
    return pairs


Z_STEPS = [moves(lambda zh, x, c, y, z, k=k: (zh, x, c, y, z ^ (1, 2)[c ^ k])) for k in (0, 1)]
Z_STEPS.append(moves(lambda zh, x, c, y, z: (zh, x, c, y, z ^ 3)))
Y_STEPS = [moves(lambda zh, x, c, y, z, k=k: (zh, x, c, y ^ (1, 3)[c ^ k], z)) for k in (0, 1)]
Y_STEPS.append(moves(lambda zh, x, c, y, z: (zh, x, c, y ^ 2, z)))
X_STEPS = [moves(lambda zh, x, c, y, z, k=k: (zh, x ^ (1, 3)[c ^ k], c, y, z)) for k in (0, 1)]
X_STEPS.append(moves(lambda zh, x, c, y, z: (zh, x ^ 2, c, y, z)))
ZH_STEP = moves(lambda zh, x, c, y, z: (zh ^ 1, x, c, y, z))
CORE_STEP = moves(lambda zh, x, c, y, z: (zh, x, c ^ 1, y, z))


def send(value, pairs):
    return lax.ppermute(value, AXES, pairs)


def join(*values):
    return jnp.concatenate(values, axis=0)


def double(value, pairs):
    return join(value, send(value, pairs))


def place():
    ctx, member = lax.axis_index("ctx"), lax.axis_index("member")
    return member % 2, ctx // 4, ctx % 4


def delta(bits, core, first, second):
    step0 = first + core * (second - first)
    step1 = second + core * (first - second)
    return (step0 if bits & 1 else 0) ^ (step1 if bits & 2 else 0)


def head_of(bits):
    core, y, _ = place()
    return y ^ delta(bits, core, 1, 3)


def columns(head, width):
    return pl.ds(pl.multiple_of(head * width, width), width)


def two_rows(pair):
    row = lax.broadcasted_iota(jnp.int32, (RIDE, HD), 0)
    wide = pair.astype(jnp.float32)
    return jnp.where(row == 0, wide[:1], jnp.where(row == 1, wide[1:], 0.0)).astype(jnp.bfloat16)


def run(copies):
    for copy in copies:
        copy.start()
    for copy in copies:
        copy.wait()


def split_kv_kernel(k_ref, v_ref, pk_ref, pv_ref, *refs):
    outs, rows, sems = refs[:4], refs[4], refs[5]
    copies = [
        pltpu.make_async_copy(pk_ref, rows.at[0], sems.at[8]),
        pltpu.make_async_copy(pv_ref, rows.at[1], sems.at[9]),
    ]
    for bits in range(4):
        part = columns(head_of(bits), HD)
        copies.append(pltpu.make_async_copy(k_ref.at[:, part], outs[bits].at[:TOK, :HD], sems.at[bits]))
        copies.append(pltpu.make_async_copy(v_ref.at[:, part], outs[bits].at[:TOK, HD:], sems.at[4 + bits]))
    run(copies)
    for bits in range(4):
        part = columns(head_of(bits), HD)
        outs[bits][TOK:, :HD] = two_rows(rows[0, :, part])
        outs[bits][TOK:, HD:] = two_rows(rows[1, :, part])


def split_kv(keys, values, prompt_keys, prompt_values):
    return pl.pallas_call(
        split_kv_kernel,
        in_specs=[HBM] * 4,
        out_specs=[VMEM] * 4,
        out_shape=[pltpu.VMEM((TOK + RIDE, 2 * HD), jnp.bfloat16)] * 4,
        scratch_shapes=[pltpu.VMEM((2, 2, KV_HEADS * HD), jnp.bfloat16), pltpu.SemaphoreType.DMA((10,))],
        name="split_kv",
    )(keys, values, prompt_keys, prompt_values)


def split_q_kernel(q_ref, *refs):
    outs, sems = refs[:4], refs[4]
    run(
        [
            pltpu.make_async_copy(q_ref.at[:, columns(head_of(bits), WIDE)], outs[bits], sems.at[bits])
            for bits in range(4)
        ]
    )


def split_q(q):
    return pl.pallas_call(
        split_q_kernel,
        in_specs=[HBM],
        out_specs=[VMEM] * 4,
        out_shape=[pltpu.VMEM((TOK, WIDE), jnp.bfloat16)] * 4,
        scratch_shapes=[pltpu.SemaphoreType.DMA((4,))],
        name="split_q",
    )(q)


def place_kernel(offsets, length, info_ref):
    core, y, z = place()
    row = lax.broadcasted_iota(jnp.int32, info_ref.shape, 0)
    info = jnp.where(row == 16, length[0], 0)
    for zbits in range(4):
        for ybits in range(4):
            source = (y ^ delta(ybits, core, 1, 3)) * 4 + (z ^ delta(zbits, core, 1, 2))
            info = jnp.where(row == zbits * 4 + ybits, offsets[0, source] * TOK, info)
    info_ref[...] = info


def places(offsets, length):
    return pl.pallas_call(
        place_kernel,
        in_specs=[SMEM, SMEM],
        out_specs=VMEM,
        out_shape=jax.ShapeDtypeStruct((24, HD), jnp.int32),
        compiler_params=pltpu.CompilerParams(vmem_limit_bytes=4 << 20),
        name="places",
    )(offsets, length)


def stack_kernel(*refs):
    parts, column_ref, sems = refs[:4], refs[4], refs[5]
    run(
        [
            pltpu.make_async_copy(parts[i].at[:TOK], column_ref.at[i * TOK : (i + 1) * TOK], sems.at[i])
            for i in range(4)
        ]
    )


def stack(parts):
    return pl.pallas_call(
        stack_kernel,
        in_specs=[pl.BlockSpec(memory_space=pl.ANY)] * 4,
        out_specs=VMEM,
        out_shape=jax.ShapeDtypeStruct((4 * TOK, 2 * HD), jnp.bfloat16),
        scratch_shapes=[pltpu.SemaphoreType.DMA((4,))],
        compiler_params=pltpu.CompilerParams(vmem_limit_bytes=4 << 20),
        name="stack",
    )(*parts)


def merge_kernel(*refs):
    parts, out_ref, sems = refs[:4], refs[4], refs[5]
    run(
        [
            pltpu.make_async_copy(parts[bits], out_ref.at[:, columns(head_of(bits), WIDE)], sems.at[bits])
            for bits in range(4)
        ]
    )


def merge(parts):
    return pl.pallas_call(
        merge_kernel,
        in_specs=[VMEM] * 4,
        out_specs=pl.BlockSpec(memory_space=pl.ANY),
        out_shape=jax.ShapeDtypeStruct((TOK, KV_HEADS * WIDE), jnp.bfloat16),
        scratch_shapes=[pltpu.SemaphoreType.DMA((4,))],
        compiler_params=pltpu.CompilerParams(vmem_limit_bytes=8 << 20),
        name="merge",
    )(*parts)


def make_kernel(queries, sizes, blocks, carried, last):
    keys = TOK * len(blocks)
    count = len(queries)

    def kernel(info_ref, *refs):
        q_refs, refs = refs[:count], refs[count:]
        pieces, refs = refs[: len(sizes)], refs[len(sizes) :]
        if carried:
            stat_in, sum_in, refs = refs[:count], refs[count : 2 * count], refs[2 * count :]
        if last:
            outs, refs = refs[:count], refs[count:]
        else:
            stat_out, sum_out, refs = refs[:count], refs[count : 2 * count], refs[2 * count :]
        k_aug, v_aug = refs
        token = lax.broadcasted_iota(jnp.int32, (TOK, TOK), 1)
        k_row = lax.broadcasted_iota(jnp.int32, (TOK, TOK), 0)

        def first_position(ybits, zbits):
            return info_ref[zbits * 4 + ybits : zbits * 4 + ybits + 1, :]

        for index, bits in enumerate(blocks):
            to = slice(index * TOK, (index + 1) * TOK)
            if bits is not None:
                k_pos = k_row + first_position(bits[0], bits[1])
            for i in range(count):
                if bits is None:
                    bias = jnp.zeros((TOK, TOK), jnp.bfloat16)
                else:
                    q_pos = token + first_position(queries[i], 0)
                    counted = (k_pos <= q_pos) & (k_pos < info_ref[16:17, :])
                    bias = jnp.where(counted, 0.0, NEG).astype(jnp.bfloat16)
                k_aug[i, to, HD:] = bias
        v_aug[:, HD:] = jnp.ones((keys, HD), jnp.bfloat16)
        start = 0
        for piece, size in zip(pieces, sizes):
            v_aug[start : start + size, :HD] = piece[:, HD:]
            for i in range(count):
                k_aug[i, start : start + size, :HD] = piece[:, :HD]
            start += size
        eye = jnp.where(token == k_row, 1.0, 0.0).astype(jnp.bfloat16)
        low = lax.broadcasted_iota(jnp.int32, (1, HD), 1) < HD // 2

        def score(i, h):
            heads = [
                jnp.concatenate([q_refs[i][:, (h * PAIR + u) * HD : (h * PAIR + u + 1) * HD], eye], axis=1)
                for u in range(PAIR)
            ]
            return lax.dot_general(
                jnp.concatenate(heads, axis=0),
                k_aug[i],
                (((1,), (1,)), ((), ())),
                preferred_element_type=jnp.float32,
            )

        def finish(i, h, s):
            top = jnp.max(s, axis=1, keepdims=True)
            if carried:
                stat = stat_in[i][h]
                before = jnp.max(jnp.where(low, stat, -3e38), axis=1, keepdims=True)
                total = jnp.max(jnp.where(low, -3e38, stat), axis=1, keepdims=True)
                top = jnp.maximum(before, top)
                rescale = jnp.exp2((before - top) * SCALE)
            weights = jnp.exp2(s * SCALE - top * SCALE).astype(jnp.bfloat16)
            both = lax.dot_general(
                weights, v_aug[...], (((1,), (0,)), ((), ())), preferred_element_type=jnp.float32
            )
            weighted, totals = both[:, :HD], both[:, HD:]
            if carried:
                weighted = weighted + sum_in[i][h] * rescale
                totals = totals + total * rescale
            if last:
                result = (weighted / totals).astype(jnp.bfloat16)
                for u in range(PAIR):
                    outs[i][:, (h * PAIR + u) * HD : (h * PAIR + u + 1) * HD] = result[u * TOK : (u + 1) * TOK]
            else:
                stat_out[i][h] = jnp.where(low, top, totals)
                sum_out[i][h] = weighted

        steps = [(i, h) for i in range(count) for h in range(PAIRS)]
        s = score(*steps[0])
        for n, step in enumerate(steps):
            ahead = score(*steps[n + 1]) if n + 1 < len(steps) else None
            finish(*step, s)
            s = ahead

    return kernel


def attend(info, queries, q, pieces, blocks, carry=(), last=False):
    sizes = [p.shape[0] for p in pieces]
    keys, count = TOK * len(blocks), len(queries)
    state = jax.ShapeDtypeStruct((PAIRS, PAIR * TOK, HD), jnp.float32)
    result = jax.ShapeDtypeStruct((TOK, WIDE), jnp.bfloat16)
    outs = [result] * count if last else [state] * (2 * count)
    return pl.pallas_call(
        make_kernel(queries, sizes, blocks, bool(carry), last),
        in_specs=[VMEM] * (1 + count + len(pieces) + len(carry)),
        out_specs=[VMEM] * len(outs),
        out_shape=outs,
        scratch_shapes=[
            pltpu.VMEM((count, keys, 2 * HD), jnp.bfloat16),
            pltpu.VMEM((keys, 2 * HD), jnp.bfloat16),
        ],
        compiler_params=pltpu.CompilerParams(vmem_limit_bytes=26 << 20),
        cost_estimate=pl.CostEstimate(
            flops=4 * WIDE * count * keys * HD, bytes_accessed=count << 20, transcendentals=WIDE * count * keys
        ),
        name="attend_last" if last else "attend_first",
    )(info, *q, *pieces, *carry)


def column_blocks(zbits):
    return [(yb, zb) for zb in zbits for yb in range(4)]


def body(
    queries, response_keys, response_values, prompt_keys, prompt_values, block_offsets, lengths
):
    mine = split_kv(response_keys[0], response_values[0], prompt_keys, prompt_values)
    queries, mine = lax.optimization_barrier((queries, mine))
    q_mine = split_q(queries[0])
    kv = [mine[0]] + [send(mine[bits], Y_STEPS[bits - 1]) for bits in (1, 2, 3)]
    column = stack(kv)
    prompt = join(*(part[TOK : TOK + 2] for part in kv))
    z_first = send(column, Z_STEPS[0])
    z_second = send(column, Z_STEPS[1])
    column, q_mine = lax.optimization_barrier((column, q_mine))
    q = [q_mine[0]] + [send(q_mine[bits], Y_STEPS[bits - 1]) for bits in (1, 2, 3)]
    prompt = double(prompt, CORE_STEP)
    block_offsets, prompt = lax.optimization_barrier((block_offsets, prompt))
    info = places(block_offsets, lengths)
    prompt = double(prompt, X_STEPS[0])
    q[1], prompt = lax.optimization_barrier((q[1], prompt))
    prompt = double(prompt, X_STEPS[1])
    z_first, z_second, prompt = lax.optimization_barrier((z_first, z_second, prompt))
    z_both = send(z_first, Z_STEPS[1])
    prompt = double(prompt, ZH_STEP)
    near = [column, z_first, z_second]

    def begin(group):
        out = attend(info, group, [q[i] for i in group], near, column_blocks((0, 1, 2)))
        return {i: [out[n], out[len(group) + n]] for n, i in enumerate(group)}

    state = begin([1, 2])
    prompts = [send(prompt, pairs) for pairs in Z_STEPS]
    state |= begin([3])
    pieces = [z_both, prompt] + prompts
    late = column_blocks((3,)) + [None] * 4
    results = [None] * 4
    for i in (3, 1, 2, 0):
        if i in state:
            out = attend(info, [i], [q[i]], pieces, late, state[i], True)[0]
        else:
            out = attend(
                info, [i], [q[i]], near + pieces, column_blocks((0, 1, 2)) + late, (), True
            )[0]
        results[i] = send(out, Y_STEPS[i - 1]) if i else out
    return merge(results)[None]


def solution(mesh):
    return jax.shard_map(
        body,
        mesh=mesh,
        in_specs=(
            P("member", "ctx", None),
            P("member", "ctx", None),
            P("member", "ctx", None),
            P(("member", "ctx"), None),
            P(("member", "ctx"), None),
            P("member", None),
            P("member"),
        ),
        out_specs=P("member", "ctx", None),
        check_vma=False,
    )
```
